512 devices in a mesh: tok: 16 (over x_lo, z), tp: 32 (over y, x_hi, core).
Axes of the slice: x: 4 (x_hi: 2, x_lo: 2; x = x_hi * 2 + x_lo), y: 8, z: 8, core: 2. Of those that a mesh axis runs over, the one named last changes fastest.
Arguments:
- activations: bfloat16 [12288, 4096], P('tok', 'tp'), may hold values from -16 to 16, as said below
- gradients: bfloat16 [12288, 4096], P('tok', 'tp'), may hold values from -16 to 16, as said below
Outputs:
- act_cov: float32 [4096, 4096], P('tp', 'tok')
- grad_cov: float32 [4096, 4096], P('tp', 'tok')
The draws below stay inside these ranges and needn't reach their ends.
Inputs may be any that keep to these rules, and one draw needn't show every extreme that they name: `activations`: Real-valued entries of order one. `gradients`: Real-valued entries of order one.
All inputs are finite; a program needn't handle non-finite values.
Results may differ from the reference program's by a relative error of at most 0.0003.
Values may be sent and summed in bfloat16 or wider, within the bound.
A program may use at most 64 MiB of HBM per device.

```python
import jax
import jax.numpy as jnp

D = 4096
TOKENS = 12288


def scaled_rows(key):
    keys = jax.random.split(key, 4)
    noise = jax.random.truncated_normal(keys[0], -4.0, 4.0, (TOKENS, D), jnp.float32)
    column = jnp.exp(jax.random.uniform(keys[2], (1, D), jnp.float32, -0.7, 0.7))
    place = jnp.arange(TOKENS, dtype=jnp.float32)[:, None] / jnp.float32(TOKENS)
    row = (0.5 + place) * jnp.exp(jax.random.uniform(keys[3], (TOKENS, 1), jnp.float32, -0.3, 0.3))
    return noise * column * row


def draw_activations(key, part):
    key = jax.random.fold_in(key, 11)
    values = scaled_rows(key)
    return values.astype(jnp.bfloat16)


def draw_gradients(key, part):
    key = jax.random.fold_in(key, 23)
    values = scaled_rows(key)
    return values.astype(jnp.bfloat16)


def setup_inputs(seed: int = 0) -> dict:
    key_of = jax.random.split(jax.random.key(seed), 3)
    return {
        "activations": draw_activations(jax.random.fold_in(key_of[2], 71), 0),
        "gradients": draw_gradients(jax.random.fold_in(key_of[2], 71), 0),
    }


def covariance(rows):
    total = jnp.dot(rows.T, rows, preferred_element_type=jnp.float32)
    return total / jnp.float32(TOKENS)


def reference(activations, gradients):
    return covariance(activations), covariance(gradients)
```

```python
import jax
import jax.numpy as jnp
from jax import lax
from jax.experimental import pallas as pl
from jax.experimental.pallas import tpu as pltpu
from jax.sharding import PartitionSpec as P

TOKENS = 768
WIDE = 128
Y = 8
Z = 8


def place(y, h, core, low, z):
    return (low * Z + z, (y * 2 + h) * 2 + core)


def kernel(
    act, grad, out_a, out_g,
    own, turned, ring, part, part4, zbuf, zbuf4, direct, mirror,
    send_x, recv_x, send_y, recv_y, send_z, recv_z, send_d, recv_d,
):
    tok, tp = lax.axis_index("tok"), lax.axis_index("tp")
    low, z = lax.div(tok, Z), lax.rem(tok, Z)
    y, h, core = lax.div(tp, 4), lax.rem(lax.div(tp, 2), 2), lax.rem(tp, 2)
    x = 2 * h + low

    def remote(src, dst, send, recv, device):
        return pltpu.make_async_remote_copy(
            src_ref=src, dst_ref=dst, send_sem=send, recv_sem=recv,
            device_id=device, device_id_type=pl.DeviceIdType.MESH,
        )

    def at_x(xx, cc):
        return place(y, lax.div(xx, 2), cc, lax.rem(xx, 2), z)

    x_up, x_down = lax.rem(x + 1, 4), lax.rem(x + 3, 4)
    y_up, y_down = lax.rem(y + 1, Y), lax.rem(y + Y - 1, Y)
    z_up, z_down = lax.rem(z + 1, Z), lax.rem(z + Z - 1, Z)
    sibling = place(y, h, 1 - core, low, z)

    barrier = pltpu.get_barrier_semaphore()
    partners = [sibling]
    partners += [at_x(xx, cc) for xx in (x_up, x_down) for cc in (0, 1)]
    partners += [place(yy, h, core, low, z) for yy in (y_up, y_down)]
    partners += [place(y, h, core, low, zz) for zz in (z_up, z_down)]
    for partner in partners:
        pl.semaphore_signal(
            barrier, inc=1, device_id=partner, device_id_type=pl.DeviceIdType.MESH
        )
    pl.semaphore_wait(barrier, len(partners))

    sends = []
    quarter = 2 * h + core
    slot, slot_sem = own.at[low, quarter], recv_x.at[low, quarter]
    for i, ref in enumerate((act, grad)):
        keep = pltpu.make_async_copy(ref, slot, slot_sem)
        give = remote(ref, slot, send_x.at[0], slot_sem, sibling)
        pl.when(core == i)(keep.start)
        pl.when(core != i)(give.start)
    sends.append(remote(act, slot, send_x.at[0], slot_sem, sibling))
    pair = 2 * h + 1 - low
    other = lax.rem(x + 3 + 2 * low, 4)
    first = jnp.where(core == low, other, pair)
    second = jnp.where(core == low, pair, other)
    for n, xx in enumerate((first, second)):
        for i, ref in enumerate((act, grad)):
            copy = remote(ref, slot, send_x.at[1 + 2 * n + i], slot_sem, at_x(xx, i))
            copy.start()
            sends.append(copy)

    def arrive(lo, q):
        pltpu.make_async_copy(own.at[lo, q], own.at[lo, q], recv_x.at[lo, q]).wait()

    def turn(lo, q):
        turned[lo, q] = own[lo, q].T

    def pass_on(source, k, xx, n):
        hh, lo = lax.div(source, 2), lax.rem(source, 2)
        ref = own.at[lo, 2 * hh + k]
        copy = remote(ref, ref, send_x.at[n], recv_x.at[lo, 2 * hh + k], at_x(xx, core))
        copy.start()
        sends.append(copy)

    q = 2 * h + low
    y_next = jnp.where(core == 0, y_down, y_up)
    halves = (low, 1 - low)

    def ring_send(step, n):
        lo = halves[n]
        src = own.at[lo, q] if step == 0 else ring.at[step - 1, lo]
        copy = remote(
            src, ring.at[step, lo], send_y.at[step, n], recv_y.at[step, lo],
            place(y_next, h, core, low, z),
        )
        copy.start()
        sends.append(copy)

    def ring_wait(step, n):
        ref = ring.at[step, halves[n]]
        pltpu.make_async_copy(ref, ref, recv_y.at[step, halves[n]]).wait()

    up_h, up_lo = lax.div(x_up, 2), lax.rem(x_up, 2)
    down_h, down_lo = lax.div(x_down, 2), lax.rem(x_down, 2)
    far = lax.rem(x + 2, 4)
    far_h, far_lo = lax.div(far, 2), lax.rem(far, 2)

    arrive(low, q)
    ring_send(0, 0)
    arrive(1 - low, q)
    ring_send(0, 1)
    arrive(low, 2 * h + 1 - low)
    turn(low, q)
    turn(low, 2 * h + 1 - low)
    ring_wait(0, 0)
    ring_send(1, 0)
    arrive(down_lo, 2 * down_h)
    pass_on(x_down, 0, x_up, 5)
    arrive(up_lo, 2 * up_h + 1)
    pass_on(x_up, 1, x_down, 6)
    ring_wait(0, 1)
    ring_send(1, 1)
    turn(down_lo, 2 * down_h)
    turn(up_lo, 2 * up_h + 1)
    ring_wait(1, 0)
    ring_send(2, 0)
    arrive(lax.rem(other, 2), 2 * lax.div(other, 2) + 1 - low)
    turn(down_lo, 2 * down_h + 1)
    turn(up_lo, 2 * up_h)
    ring_wait(1, 1)
    ring_send(2, 1)
    for k in (0, 1):
        arrive(far_lo, 2 * far_h + k)
        turn(far_lo, 2 * far_h + k)

    a4 = jnp.where(y < Y // 2, h, 1 - h)

    def product(d):
        def term(lo):
            right = own[lo, q] if d == 0 else ring[d - 1, lo]
            if d < 4:
                left = turned[lo].reshape(4 * WIDE, TOKENS)
            else:
                left = turned[lo, pl.ds(2 * a4, 2)].reshape(2 * WIDE, TOKENS)
            return jnp.dot(left, right, preferred_element_type=jnp.float32)

        total = term(0) + term(1)
        if d < 4:
            part[d] = total
        else:
            part4[...] = total

    def held(d):
        if d < 4:
            return part.at[d], zbuf.at[d], 64
        return part4, zbuf4, 32

    arriving = {}

    def z_step(d, s):
        mine, buf, n = held(d)
        for way in (0, 1):
            shift = Z + 4 - s if way else Z - (4 - s)
            base = lax.rem(z + shift, Z) * n
            lo, count = way * (n // 2), n // 2
            if s > 0:
                arriving[d, way, s - 1].wait_recv()
                if s > 1:
                    lo, count = 0, n
                at = pl.ds(pl.multiple_of(base + lo, 8), count)
                mine[at, :] += buf[way, s - 1, lo : lo + count]
                lo, count = 0, n
            copy = remote(
                mine.at[pl.ds(pl.multiple_of(base + lo, 8), count)],
                buf.at[way, s, pl.ds(lo, count)],
                send_z.at[d, way, s], recv_z.at[d, way, s],
                place(y, h, core, low, z_up if way else z_down),
            )
            copy.start()
            arriving[d, way, s] = copy
            sends.append(copy)

    kept = []

    def deliver(d):
        mine, buf, n = held(d)
        here = pl.ds(pl.multiple_of(z * n, 8), n)
        for way in (0, 1):
            arriving[d, way, 3].wait_recv()
        mine[here, :] += buf[0, 3] + buf[1, 3]
        yq = lax.rem(y + Y + jnp.where(core == 0, d, -d), Y)
        t1 = 2 * yq + h
        if d < 4:
            a, kk = lax.div(z, 4), lax.rem(lax.div(z, 2), 2)
            row1, row2 = lax.rem(z, 2) * n, lax.rem(z, 4) * n
        else:
            a, kk = a4, lax.div(z, 4)
            row1, row2 = lax.rem(z, 4) * n, z * n
        dst = direct.at[
            core,
            pl.ds(pl.multiple_of(row1, 8), n),
            pl.ds(pl.multiple_of(low * WIDE, WIDE), WIDE),
        ]
        is_self = (a == h) & (kk == core) & (t1 == tok)
        copy = remote(
            mine.at[here], dst, send_d.at[d, 0], recv_d.at[core],
            place(y, a, kk, lax.div(t1, Z), lax.rem(t1, Z)),
        )
        local = pltpu.make_async_copy(mine.at[here], dst, recv_d.at[core])
        pl.when(jnp.logical_not(is_self))(copy.start)
        pl.when(is_self)(local.start)
        kept.append((jnp.logical_not(is_self), copy))
        if d > 0:
            t2 = 2 * y + a
            copy = remote(
                mine.at[here],
                mirror.at[core, pl.ds(pl.multiple_of(row2, 8), n)],
                send_d.at[d, 1], recv_d.at[core],
                place(yq, h, low, lax.div(t2, Z), lax.rem(t2, Z)),
            )
            copy.start()
            sends.append(copy)

    product(0)
    z_step(0, 0)
    product(1)
    z_step(1, 0)
    ring_wait(2, 0)
    ring_send(3, 0)
    z_step(0, 1)
    product(2)
    z_step(2, 0)
    z_step(1, 1)
    ring_wait(2, 1)
    ring_send(3, 1)
    z_step(0, 2)
    product(3)
    z_step(3, 0)
    z_step(2, 1)
    z_step(1, 2)
    z_step(0, 3)
    ring_wait(3, 0)
    ring_wait(3, 1)
    product(4)
    z_step(4, 0)
    z_step(3, 1)
    z_step(2, 2)
    z_step(1, 3)
    deliver(0)
    z_step(4, 1)
    z_step(3, 2)
    z_step(2, 3)
    deliver(1)
    z_step(4, 2)
    z_step(3, 3)
    deliver(2)
    z_step(4, 3)
    deliver(3)
    deliver(4)

    scale = jnp.float32(1.0 / (TOKENS * 2 * Z))
    y2, h2 = lax.div(tok, 2), lax.rem(tok, 2)
    on_time = jnp.where(y < Y // 2, h == h2, h != h2)
    for i, out in enumerate((out_a, out_g)):
        d = lax.rem((y2 - y if i == 0 else y - y2) + Y, Y)
        straight = (d < 4) | ((d == 4) & on_time)

        @pl.when(straight)
        def _():
            ref = direct.at[i]
            pltpu.make_async_copy(ref, ref, recv_d.at[i]).wait()
            out[...] = direct[i] * scale

        @pl.when(jnp.logical_not(straight))
        def _():
            ref = mirror.at[i]
            pltpu.make_async_copy(ref, ref, recv_d.at[i]).wait()
            out[...] = mirror[i].T * scale

    for copy in sends:
        copy.wait_send()
    for remote_one, copy in kept:
        pl.when(remote_one)(copy.wait_send)


def per_device(activations, gradients):
    vmem, sem = pltpu.VMEM, pltpu.SemaphoreType.DMA
    block = jax.ShapeDtypeStruct((WIDE, 2 * WIDE), jnp.float32)
    return pl.pallas_call(
        kernel,
        out_shape=(block, block),
        in_specs=[pl.BlockSpec(memory_space=pl.ANY)] * 2,
        out_specs=[pl.BlockSpec(memory_space=pltpu.VMEM)] * 2,
        scratch_shapes=[
            vmem((2, 4, TOKENS, WIDE), jnp.bfloat16),
            vmem((2, 4, WIDE, TOKENS), jnp.bfloat16),
            vmem((4, 2, TOKENS, WIDE), jnp.bfloat16),
            vmem((4, 4 * WIDE, WIDE), jnp.float32),
            vmem((2 * WIDE, WIDE), jnp.float32),
            vmem((4, 2, 4, 64, WIDE), jnp.float32),
            vmem((2, 4, 32, WIDE), jnp.float32),
            vmem((2, WIDE, 2 * WIDE), jnp.float32),
            vmem((2, 2 * WIDE, WIDE), jnp.float32),
            sem((7,)), sem((2, 4)),
            sem((4, 2)), sem((4, 2)),
            sem((5, 2, 4)), sem((5, 2, 4)),
            sem((5, 2)), sem((2,)),
        ],
        compiler_params=pltpu.CompilerParams(
            collective_id=0, has_side_effects=True, vmem_limit_bytes=40 * 2**20
        ),
        cost_estimate=pl.CostEstimate(
            flops=2 * 2304 * 1536 * 128, bytes_accessed=2**20, transcendentals=0
        ),
    )(activations, gradients)


def solution(mesh):
    placed = (P("tok", "tp"), P("tok", "tp"))
    return jax.shard_map(
        per_device,
        mesh=mesh,
        in_specs=placed,
        out_specs=(P("tp", "tok"), P("tp", "tok")),
        check_vma=False,
    )
```

```python
import jax
import jax.numpy as jnp
from jax import lax
from jax.experimental import pallas as pl
from jax.experimental.pallas import tpu as pltpu
from jax.sharding import PartitionSpec as P

TOKENS = 768
WIDE = 128
HALF = TOKENS // 2
CHUNK = 32
Y = 8
Z = 8


def place(y, h, core, low, z):
    return (low * Z + z, (y * 2 + h) * 2 + core)


def kernel(
    act, grad, out_a, out_g,
    own, turned, ring, part, zbuf, direct, mirror,
    send_x, recv_x, send_y, recv_y, send_z, recv_z, send_d, recv_d,
):
    tok, tp = lax.axis_index("tok"), lax.axis_index("tp")
    low, z = lax.div(tok, Z), lax.rem(tok, Z)
    y, h, core = lax.div(tp, 4), lax.rem(lax.div(tp, 2), 2), lax.rem(tp, 2)
    x = 2 * h + low

    def remote(src, dst, send, recv, device):
        return pltpu.make_async_remote_copy(
            src_ref=src, dst_ref=dst, send_sem=send, recv_sem=recv,
            device_id=device, device_id_type=pl.DeviceIdType.MESH,
        )

    def at_x(xx, cc):
        return place(y, lax.div(xx, 2), cc, lax.rem(xx, 2), z)

    x_up, x_down = lax.rem(x + 1, 4), lax.rem(x + 3, 4)
    y_up, y_down = lax.rem(y + 1, Y), lax.rem(y + Y - 1, Y)
    z_up, z_down = lax.rem(z + 1, Z), lax.rem(z + Z - 1, Z)
    sibling = place(y, h, 1 - core, low, z)

    barrier = pltpu.get_barrier_semaphore()
    partners = [sibling]
    partners += [at_x(xx, cc) for xx in (x_up, x_down) for cc in (0, 1)]
    partners += [place(yy, h, core, low, z) for yy in (y_up, y_down)]
    partners += [place(y, h, core, low, zz) for zz in (z_up, z_down)]
    for partner in partners:
        pl.semaphore_signal(
            barrier, inc=1, device_id=partner, device_id_type=pl.DeviceIdType.MESH
        )
    pl.semaphore_wait(barrier, len(partners))

    sends = []
    quarter = 2 * h + core
    pair = 2 * h + 1 - low
    other = lax.rem(x + 3 + 2 * low, 4)
    far = lax.rem(x + 2, 4)
    inputs = (act, grad)

    def piece(ref, part_of):
        return ref.at[pl.ds(part_of * HALF, HALF)]

    for half in (0, 1):
        dst = piece(own.at[low, quarter], half)
        sem = recv_x.at[low, quarter, half]
        for i, ref in enumerate(inputs):
            keep = pltpu.make_async_copy(piece(ref, half), dst, sem)
            give = remote(piece(ref, half), dst, send_x.at[0, half], sem, sibling)
            pl.when(core == i)(keep.start)
            pl.when(core != i)(give.start)
        sends.append(remote(piece(act, half), dst, send_x.at[0, half], sem, sibling))
    first = jnp.where(core == low, other, pair)
    second = jnp.where(core == low, pair, other)

    def x_send(n, half):
        for i, ref in enumerate(inputs):
            copy = remote(
                piece(ref, half), piece(own.at[low, quarter], half),
                send_x.at[1 + 2 * n + i, half], recv_x.at[low, quarter, half],
                at_x(second if n else first, i),
            )
            copy.start()
            sends.append(copy)

    x_send(0, 0)
    x_send(0, 1)

    def slot_of(chip, k):
        return lax.rem(chip, 2), 2 * lax.div(chip, 2) + k

    def arrive(chip, k, half):
        lo, qq = slot_of(chip, k)
        ref = piece(own.at[lo, qq], half)
        pltpu.make_async_copy(ref, ref, recv_x.at[lo, qq, half]).wait()

    def turn(chip):
        for k in (0, 1):
            lo, qq = slot_of(chip, k)
            turned[lo, qq] = own[lo, qq].T

    def pass_on(half, origin, k, to, n):
        lo, qq = slot_of(origin, k)
        ref = piece(own.at[lo, qq], half)
        copy = remote(ref, ref, send_x.at[n, half], recv_x.at[lo, qq, half], at_x(to, core))
        copy.start()
        sends.append(copy)

    q = 2 * h + low
    y_next = jnp.where(core == 0, y_down, y_up)
    groups = (low, 1 - low)

    def ring_piece(step, n, half):
        lo = groups[n]
        if step < 0:
            return piece(own.at[lo, q], half)
        return piece(ring.at[step, lo], half)

    def ring_wait(step, n, half):
        ref = ring_piece(step, n, half)
        pltpu.make_async_copy(ref, ref, recv_y.at[step, groups[n], half]).wait()

    def y_send(step, n, half):
        if step > 0:
            ring_wait(step - 1, n, half)
        copy = remote(
            ring_piece(step - 1, n, half), ring_piece(step, n, half),
            send_y.at[step, n, half], recv_y.at[step, groups[n], half],
            place(y_next, h, core, low, z),
        )
        copy.start()
        sends.append(copy)

    def product(d):
        def term(lo):
            right = own[lo, q] if d == 0 else ring[d - 1, lo]
            left = turned[lo].reshape(4 * WIDE, TOKENS)
            return jnp.dot(left, right, preferred_element_type=jnp.float32)

        part[d] = (term(0) + term(1)).reshape(2, 2 * WIDE, WIDE)

    arriving = {}

    def z_step(d, s):
        mine, buf = part.at[d], zbuf.at[d]
        for way in (0, 1):
            shift = Z + 4 - s if way else Z - (4 - s)
            base = lax.rem(z + shift, Z) * CHUNK
            lo, count = way * (CHUNK // 2), CHUNK // 2
            if s > 0:
                arriving[d, way, s - 1].wait_recv()
                if s > 1:
                    lo, count = 0, CHUNK
                at = pl.ds(pl.multiple_of(base + lo, 8), count)
                mine[:, at, :] += buf[way, s - 1, :, lo : lo + count]
                lo, count = 0, CHUNK
            copy = remote(
                mine.at[:, pl.ds(pl.multiple_of(base + lo, 8), count)],
                buf.at[way, s, :, pl.ds(lo, count)],
                send_z.at[d, way, s], recv_z.at[d, way, s],
                place(y, h, core, low, z_up if way else z_down),
            )
            copy.start()
            arriving[d, way, s] = copy
            sends.append(copy)

    kept = []

    def deliver(d):
        mine, buf = part.at[d], zbuf.at[d]
        here = pl.ds(pl.multiple_of(z * CHUNK, CHUNK), CHUNK)
        for way in (0, 1):
            arriving[d, way, 3].wait_recv()
        mine[:, here, :] += buf[0, 3] + buf[1, 3]
        yq = lax.rem(y + Y + jnp.where(core == 0, d, -d), Y)
        t1 = 2 * yq + h
        kk, row = lax.div(z, 4), lax.rem(z, 4) * CHUNK
        for a in (0, 1):
            dst = direct.at[
                core,
                pl.ds(pl.multiple_of(row, CHUNK), CHUNK),
                pl.ds(pl.multiple_of(low * WIDE, WIDE), WIDE),
            ]
            is_self = (a == h) & (kk == core) & (t1 == tok)
            copy = remote(
                mine.at[a, here], dst, send_d.at[d, a, 0], recv_d.at[core],
                place(y, a, kk, lax.div(t1, Z), lax.rem(t1, Z)),
            )
            local = pltpu.make_async_copy(mine.at[a, here], dst, recv_d.at[core])
            pl.when(jnp.logical_not(is_self))(copy.start)
            pl.when(is_self)(local.start)
            kept.append((jnp.logical_not(is_self), copy))
            if 0 < d < 4:
                t2 = 2 * y + a
                copy = remote(
                    mine.at[a, here],
                    mirror.at[core, here],
                    send_d.at[d, a, 1], recv_d.at[core],
                    place(yq, h, low, lax.div(t2, Z), lax.rem(t2, Z)),
                )
                copy.start()
                sends.append(copy)

    arrive(x, low, 0)
    arrive(x, low, 1)
    arrive(x, 1 - low, 0)
    arrive(x, 1 - low, 1)
    turn(x)
    y_send(0, 0, 0)
    y_send(0, 0, 1)
    arrive(pair, low, 0)
    y_send(0, 1, 0)
    x_send(1, 0)
    pass_on(0, pair, low, other, 5)
    arrive(other, 1 - low, 0)
    pass_on(0, other, 1 - low, pair, 6)
    y_send(1, 0, 0)
    y_send(1, 0, 1)
    arrive(pair, low, 1)
    y_send(0, 1, 1)
    x_send(1, 1)
    pass_on(1, pair, low, other, 5)
    arrive(other, 1 - low, 1)
    pass_on(1, other, 1 - low, pair, 6)
    y_send(1, 1, 0)
    y_send(2, 0, 0)
    y_send(2, 0, 1)
    y_send(1, 1, 1)
    y_send(2, 1, 0)
    y_send(3, 0, 0)
    arrive(other, low, 0)
    arrive(other, low, 1)
    turn(other)
    arrive(pair, 1 - low, 0)
    arrive(pair, 1 - low, 1)
    turn(pair)
    y_send(3, 0, 1)
    y_send(2, 1, 1)
    arrive(far, low, 0)
    arrive(far, low, 1)
    arrive(far, 1 - low, 0)
    arrive(far, 1 - low, 1)
    turn(far)
    product(0)
    z_step(0, 0)
    y_send(3, 1, 0)
    product(1)
    z_step(1, 0)
    product(2)
    z_step(2, 0)
    z_step(0, 1)
    y_send(3, 1, 1)
    z_step(1, 1)
    product(3)
    z_step(3, 0)
    z_step(2, 1)
    z_step(0, 2)
    ring_wait(3, 0, 0)
    ring_wait(3, 0, 1)
    ring_wait(3, 1, 0)
    ring_wait(3, 1, 1)
    product(4)
    z_step(4, 0)
    z_step(1, 2)
    z_step(3, 1)
    z_step(2, 2)
    z_step(0, 3)
    z_step(4, 1)
    z_step(1, 3)
    z_step(3, 2)
    z_step(2, 3)
    early = len(sends)
    deliver(0)
    z_step(4, 2)
    deliver(1)
    z_step(3, 3)
    deliver(2)
    z_step(4, 3)
    deliver(3)
    deliver(4)

    for copy in sends[:early]:
        copy.wait_send()
    scale = jnp.float32(1.0 / (TOKENS * 2 * Z))
    y2 = lax.div(tok, 2)
    for i, out in enumerate((out_a, out_g)):
        d = lax.rem((y2 - y if i == 0 else y - y2) + Y, Y)
        straight = d <= 4

        @pl.when(straight)
        def _():
            ref = direct.at[i]
            pltpu.make_async_copy(ref, ref, recv_d.at[i]).wait()
            out[...] = direct[i] * scale

        @pl.when(jnp.logical_not(straight))
        def _():
            ref = mirror.at[i]
            pltpu.make_async_copy(ref, ref, recv_d.at[i]).wait()
            out[...] = mirror[i].T * scale

    for copy in sends[early:]:
        copy.wait_send()
    for remote_one, copy in kept:
        pl.when(remote_one)(copy.wait_send)


def per_device(activations, gradients):
    vmem, sem = pltpu.VMEM, pltpu.SemaphoreType.DMA
    block = jax.ShapeDtypeStruct((WIDE, 2 * WIDE), jnp.float32)
    return pl.pallas_call(
        kernel,
        out_shape=(block, block),
        in_specs=[pl.BlockSpec(memory_space=pl.ANY)] * 2,
        out_specs=[pl.BlockSpec(memory_space=pltpu.VMEM)] * 2,
        scratch_shapes=[
            vmem((2, 4, TOKENS, WIDE), jnp.bfloat16),
            vmem((2, 4, WIDE, TOKENS), jnp.bfloat16),
            vmem((4, 2, TOKENS, WIDE), jnp.bfloat16),
            vmem((5, 2, 2 * WIDE, WIDE), jnp.float32),
            vmem((5, 2, 4, 2, CHUNK, WIDE), jnp.float32),
            vmem((2, WIDE, 2 * WIDE), jnp.float32),
            vmem((2, 2 * WIDE, WIDE), jnp.float32),
            sem((7, 2)), sem((2, 4, 2)),
            sem((4, 2, 2)), sem((4, 2, 2)),
            sem((5, 2, 4)), sem((5, 2, 4)),
            sem((5, 2, 2)), sem((2,)),
        ],
        compiler_params=pltpu.CompilerParams(
            collective_id=0, has_side_effects=True, vmem_limit_bytes=54840 * 2**10
        ),
        cost_estimate=pl.CostEstimate(
            flops=2 * 2560 * 1536 * 128, bytes_accessed=2**20, transcendentals=0
        ),
    )(activations, gradients)


def solution(mesh):
    placed = (P("tok", "tp"), P("tok", "tp"))
    return jax.shard_map(
        per_device,
        mesh=mesh,
        in_specs=placed,
        out_specs=(P("tp", "tok"), P("tp", "tok")),
        check_vma=False,
    )
```

```python
import jax
import jax.numpy as jnp
from jax import lax
from jax.experimental import pallas as pl
from jax.experimental.pallas import tpu as pltpu
from jax.sharding import PartitionSpec as P

TOKENS = 768
WIDE = 128
HALF = TOKENS // 2
NEAR, FAR, BOTH = 0, 1, 2
CHUNK = 32
Y = 8
Z = 8


def place(y, h, core, low, z):
    return (low * Z + z, (y * 2 + h) * 2 + core)


def kernel(
    act, grad, out_a, out_g,
    own, turned, ring, part, coded, cbuf, direct, mirror,
    send_x, recv_x, send_y, recv_y, near, send_c, recv_c, send_d, recv_d,
):
    tok, tp = lax.axis_index("tok"), lax.axis_index("tp")
    low, z = lax.div(tok, Z), lax.rem(tok, Z)
    y, h, core = lax.div(tp, 4), lax.rem(lax.div(tp, 2), 2), lax.rem(tp, 2)
    x = 2 * h + low

    def remote(src, dst, send, recv, device):
        return pltpu.make_async_remote_copy(
            src_ref=src, dst_ref=dst, send_sem=send, recv_sem=recv,
            device_id=device, device_id_type=pl.DeviceIdType.MESH,
        )

    def at_x(xx, cc):
        return place(y, lax.div(xx, 2), cc, lax.rem(xx, 2), z)

    x_up, x_down = lax.rem(x + 1, 4), lax.rem(x + 3, 4)
    y_up, y_down = lax.rem(y + 1, Y), lax.rem(y + Y - 1, Y)
    z_up, z_down = lax.rem(z + 1, Z), lax.rem(z + Z - 1, Z)
    sibling = place(y, h, 1 - core, low, z)

    barrier = pltpu.get_barrier_semaphore()
    partners = [sibling]
    partners += [at_x(xx, cc) for xx in (x_up, x_down) for cc in (0, 1)]
    partners += [place(yy, h, core, low, z) for yy in (y_up, y_down)]
    partners += [place(y, h, core, low, zz) for zz in (z_up, z_down)]
    for partner in partners:
        pl.semaphore_signal(
            barrier, inc=1, device_id=partner, device_id_type=pl.DeviceIdType.MESH
        )
    pl.semaphore_wait(barrier, len(partners))

    sends = []
    quarter = 2 * h + core
    pair = 2 * h + 1 - low
    other = lax.rem(x + 3 + 2 * low, 4)
    far = lax.rem(x + 2, 4)
    inputs = (act, grad)

    def piece(ref, part_of):
        return ref.at[pl.ds(part_of * HALF, HALF)]

    for half in (0, 1):
        dst = piece(own.at[low, quarter], half)
        sem = recv_x.at[low, quarter, half]
        for i, ref in enumerate(inputs):
            keep = pltpu.make_async_copy(piece(ref, half), dst, sem)
            give = remote(piece(ref, half), dst, send_x.at[0, half], sem, sibling)
            pl.when(core == i)(keep.start)
            pl.when(core != i)(give.start)
        sends.append(remote(piece(act, half), dst, send_x.at[0, half], sem, sibling))
    first = jnp.where(core == low, other, pair)
    second = jnp.where(core == low, pair, other)

    def x_send(n, half):
        for i, ref in enumerate(inputs):
            copy = remote(
                piece(ref, half), piece(own.at[low, quarter], half),
                send_x.at[1 + 2 * n + i, half], recv_x.at[low, quarter, half],
                at_x(second if n else first, i),
            )
            copy.start()
            sends.append(copy)

    x_send(0, 0)
    x_send(0, 1)

    def slot_of(chip, k):
        return lax.rem(chip, 2), 2 * lax.div(chip, 2) + k

    def arrive(chip, k, half):
        lo, qq = slot_of(chip, k)
        ref = piece(own.at[lo, qq], half)
        pltpu.make_async_copy(ref, ref, recv_x.at[lo, qq, half]).wait()

    def turn(chip):
        for k in (0, 1):
            lo, qq = slot_of(chip, k)
            turned[lo, qq] = own[lo, qq].T

    def pass_on(half, origin, k, to, n):
        lo, qq = slot_of(origin, k)
        ref = piece(own.at[lo, qq], half)
        copy = remote(ref, ref, send_x.at[n, half], recv_x.at[lo, qq, half], at_x(to, core))
        copy.start()
        sends.append(copy)

    q = 2 * h + low
    y_next = jnp.where(core == 0, y_down, y_up)
    groups = (low, 1 - low)

    def ring_piece(step, n, half):
        lo = groups[n]
        if step < 0:
            return piece(own.at[lo, q], half)
        return piece(ring.at[step, lo], half)

    def ring_wait(step, n, half):
        ref = ring_piece(step, n, half)
        pltpu.make_async_copy(ref, ref, recv_y.at[step, groups[n], half]).wait()

    def y_send(step, n, half):
        if step > 0:
            ring_wait(step - 1, n, half)
        copy = remote(
            ring_piece(step - 1, n, half), ring_piece(step, n, half),
            send_y.at[step, n, half], recv_y.at[step, groups[n], half],
            place(y_next, h, core, low, z),
        )
        copy.start()
        sends.append(copy)

    def rows_of(unit):
        if unit == BOTH:
            return 0, 2
        return (h if unit == NEAR else 1 - h), 1

    def product(d, unit):
        first, count = rows_of(unit)

        def term(lo):
            right = own[lo, q] if d == 0 else ring[d - 1, lo]
            left = turned[lo, pl.ds(2 * first, 2 * count)]
            left = left.reshape(2 * count * WIDE, TOKENS)
            return jnp.dot(left, right, preferred_element_type=jnp.float32)

        total = term(0) + term(1)
        part[d, pl.ds(first, count)] = total.reshape(count, 2 * WIDE, WIDE)

    arriving = {}

    def greet(n):
        for way, zz in enumerate((z_up, z_down)):
            pl.semaphore_signal(
                near.at[n, way], inc=1, device_id=place(y, h, core, low, zz),
                device_id_type=pl.DeviceIdType.MESH,
            )

    def greeted(n):
        for way in (0, 1):
            pl.semaphore_wait(near.at[n, way], 1)

    def scatter(d, unit):
        side = pl.ds(*rows_of(unit))
        term = part[d, side] * 0.0625
        square = term * term
        power = term * jnp.abs(term) * square * (square * square)
        coded[d, side] = power.astype(jnp.bfloat16)
        for o in (4, 3, 5, 2, 6, 1, 7):
            zz = lax.rem(z + o, Z)
            copy = remote(
                coded.at[d, side, pl.ds(pl.multiple_of(zz * CHUNK, CHUNK), CHUNK)],
                cbuf.at[d, o - 1, side],
                send_c.at[d, unit, o - 1], recv_c.at[d, unit, o - 1],
                place(y, h, core, low, zz),
            )
            copy.start()
            arriving[d, unit, o] = copy
            sends.append(copy)

    def gathered(d, unit):
        side = pl.ds(*rows_of(unit))
        total = 0.0
        for o in (1, 7, 2, 6, 3, 5, 4):
            arriving[d, unit, o].wait_recv()
            power = cbuf[d, o - 1, side].astype(jnp.float32)
            root = jnp.sqrt(jnp.sqrt(jnp.sqrt(jnp.abs(power))))
            total += jnp.where(power < 0.0, -root, root)
        return total * 16.0

    kept = []

    def deliver(d, unit):
        first, count = rows_of(unit)
        mine = part.at[d]
        here = pl.ds(pl.multiple_of(z * CHUNK, CHUNK), CHUNK)
        mine[pl.ds(first, count), here, :] += gathered(d, unit)
        yq = lax.rem(y + Y + jnp.where(core == 0, d, -d), Y)
        t1 = 2 * yq + h
        kk, row = lax.div(z, 4), lax.rem(z, 4) * CHUNK
        for n in range(count):
            a = first + n
            dst = direct.at[
                core,
                pl.ds(pl.multiple_of(row, CHUNK), CHUNK),
                pl.ds(pl.multiple_of(low * WIDE, WIDE), WIDE),
            ]
            is_self = (a == h) & (kk == core) & (t1 == tok)
            copy = remote(
                mine.at[a, here], dst, send_d.at[d, unit + n, 0], recv_d.at[core],
                place(y, a, kk, lax.div(t1, Z), lax.rem(t1, Z)),
            )
            local = pltpu.make_async_copy(mine.at[a, here], dst, recv_d.at[core])
            pl.when(jnp.logical_not(is_self))(copy.start)
            pl.when(is_self)(local.start)
            kept.append((jnp.logical_not(is_self), copy))
            if 0 < d < 4:
                t2 = 2 * y + a
                copy = remote(
                    mine.at[a, here],
                    mirror.at[core, here],
                    send_d.at[d, unit + n, 1], recv_d.at[core],
                    place(yq, h, low, lax.div(t2, Z), lax.rem(t2, Z)),
                )
                copy.start()
                sends.append(copy)

    greet(0)
    arrive(x, low, 0)
    arrive(x, low, 1)
    arrive(x, 1 - low, 0)
    arrive(x, 1 - low, 1)
    turn(x)
    y_send(0, 0, 0)
    y_send(0, 0, 1)
    arrive(pair, low, 0)
    greeted(0)
    greet(1)
    y_send(0, 1, 0)
    x_send(1, 0)
    pass_on(0, pair, low, other, 5)
    arrive(other, 1 - low, 0)
    pass_on(0, other, 1 - low, pair, 6)
    y_send(1, 0, 0)
    y_send(1, 0, 1)
    arrive(pair, low, 1)
    y_send(0, 1, 1)
    x_send(1, 1)
    pass_on(1, pair, low, other, 5)
    arrive(other, 1 - low, 1)
    greeted(1)
    greet(2)
    pass_on(1, other, 1 - low, pair, 6)
    y_send(1, 1, 0)
    y_send(2, 0, 0)
    y_send(2, 0, 1)
    y_send(1, 1, 1)
    y_send(2, 1, 0)
    y_send(3, 0, 0)
    arrive(pair, 1 - low, 0)
    arrive(pair, 1 - low, 1)
    turn(pair)
    greeted(2)
    product(0, NEAR)
    scatter(0, NEAR)
    product(1, NEAR)
    scatter(1, NEAR)
    y_send(3, 0, 1)
    y_send(2, 1, 1)
    product(2, NEAR)
    scatter(2, NEAR)
    arrive(other, low, 0)
    arrive(other, low, 1)
    turn(other)
    arrive(far, low, 0)
    arrive(far, low, 1)
    arrive(far, 1 - low, 0)
    arrive(far, 1 - low, 1)
    turn(far)
    product(0, FAR)
    scatter(0, FAR)
    y_send(3, 1, 0)
    y_send(3, 1, 1)
    product(1, FAR)
    scatter(1, FAR)
    product(2, FAR)
    scatter(2, FAR)
    product(3, BOTH)
    scatter(3, BOTH)
    ring_wait(3, 0, 0)
    ring_wait(3, 0, 1)
    ring_wait(3, 1, 0)
    ring_wait(3, 1, 1)
    product(4, BOTH)
    scatter(4, BOTH)
    deliver(0, NEAR)
    deliver(1, NEAR)
    deliver(2, NEAR)
    deliver(0, FAR)
    deliver(1, FAR)
    deliver(2, FAR)
    deliver(3, BOTH)
    deliver(4, BOTH)

    scale = jnp.float32(1.0 / (TOKENS * 2 * Z))
    y2 = lax.div(tok, 2)
    for i, out in enumerate((out_a, out_g)):
        d = lax.rem((y2 - y if i == 0 else y - y2) + Y, Y)
        straight = d <= 4

        @pl.when(straight)
        def _():
            ref = direct.at[i]
            pltpu.make_async_copy(ref, ref, recv_d.at[i]).wait()
            out[...] = direct[i] * scale

        @pl.when(jnp.logical_not(straight))
        def _():
            ref = mirror.at[i]
            pltpu.make_async_copy(ref, ref, recv_d.at[i]).wait()
            out[...] = mirror[i].T * scale

    for copy in sends:
        copy.wait_send()
    for remote_one, copy in kept:
        pl.when(remote_one)(copy.wait_send)


def per_device(activations, gradients):
    vmem, sem = pltpu.VMEM, pltpu.SemaphoreType.DMA
    block = jax.ShapeDtypeStruct((WIDE, 2 * WIDE), jnp.float32)
    return pl.pallas_call(
        kernel,
        out_shape=(block, block),
        in_specs=[pl.BlockSpec(memory_space=pl.ANY)] * 2,
        out_specs=[pl.BlockSpec(memory_space=pltpu.VMEM)] * 2,
        scratch_shapes=[
            vmem((2, 4, TOKENS, WIDE), jnp.bfloat16),
            vmem((2, 4, WIDE, TOKENS), jnp.bfloat16),
            vmem((4, 2, TOKENS, WIDE), jnp.bfloat16),
            vmem((5, 2, 2 * WIDE, WIDE), jnp.float32),
            vmem((5, 2, 2 * WIDE, WIDE), jnp.bfloat16),
            vmem((5, 7, 2, CHUNK, WIDE), jnp.bfloat16),
            vmem((2, WIDE, 2 * WIDE), jnp.float32),
            vmem((2, 2 * WIDE, WIDE), jnp.float32),
            sem((7, 2)), sem((2, 4, 2)),
            sem((4, 2, 2)), sem((4, 2, 2)),
            pltpu.SemaphoreType.REGULAR((3, 2)),
            sem((5, 3, 7)), sem((5, 3, 7)),
            sem((5, 4, 2)), sem((2,)),
        ],
        compiler_params=pltpu.CompilerParams(
            collective_id=0, has_side_effects=True, vmem_limit_bytes=54840 * 2**10
        ),
        cost_estimate=pl.CostEstimate(
            flops=2 * 2560 * 1536 * 128, bytes_accessed=2**20, transcendentals=0
        ),
    )(activations, gradients)


def solution(mesh):
    placed = (P("tok", "tp"), P("tok", "tp"))
    return jax.shard_map(
        per_device,
        mesh=mesh,
        in_specs=placed,
        out_specs=(P("tp", "tok"), P("tp", "tok")),
        check_vma=False,
    )
```

```python
import jax
import jax.numpy as jnp
from jax import lax
from jax.experimental import pallas as pl
from jax.experimental.pallas import tpu as pltpu
from jax.sharding import PartitionSpec as P

TOKENS = 768
WIDE = 128
HALF = TOKENS // 2
NEAR, FAR, BOTH = 0, 1, 2
CHUNK = 32
Y = 8
Z = 8


def place(y, h, core, low, z):
    return (low * Z + z, (y * 2 + h) * 2 + core)


def kernel(
    act, grad, out_a, out_g,
    own, turned, ring, part, coded, cbuf, direct, mirror,
    send_x, recv_x, send_y, recv_y, near, send_c, recv_c, send_d, recv_d,
):
    tok, tp = lax.axis_index("tok"), lax.axis_index("tp")
    low, z = lax.div(tok, Z), lax.rem(tok, Z)
    y, h, core = lax.div(tp, 4), lax.rem(lax.div(tp, 2), 2), lax.rem(tp, 2)
    x = 2 * h + low

    def remote(src, dst, send, recv, device):
        return pltpu.make_async_remote_copy(
            src_ref=src, dst_ref=dst, send_sem=send, recv_sem=recv,
            device_id=device, device_id_type=pl.DeviceIdType.MESH,
        )

    def at_x(xx, cc):
        return place(y, lax.div(xx, 2), cc, lax.rem(xx, 2), z)

    x_up, x_down = lax.rem(x + 1, 4), lax.rem(x + 3, 4)
    y_up, y_down = lax.rem(y + 1, Y), lax.rem(y + Y - 1, Y)
    z_up, z_down = lax.rem(z + 1, Z), lax.rem(z + Z - 1, Z)
    sibling = place(y, h, 1 - core, low, z)

    barrier = pltpu.get_barrier_semaphore()
    partners = [sibling]
    partners += [at_x(xx, cc) for xx in (x_up, x_down) for cc in (0, 1)]
    partners += [place(yy, h, cc, low, z) for yy in (y_up, y_down) for cc in (0, 1)]
    partners += [place(y, h, core, low, zz) for zz in (z_up, z_down)]
    for partner in partners:
        pl.semaphore_signal(
            barrier, inc=1, device_id=partner, device_id_type=pl.DeviceIdType.MESH
        )
    pl.semaphore_wait(barrier, len(partners))

    quarter = 2 * h + core
    pair = 2 * h + 1 - low
    other = lax.rem(x + 3 + 2 * low, 4)
    far = lax.rem(x + 2, 4)
    inputs = (act, grad)

    def piece(ref, part_of):
        return ref.at[pl.ds(part_of * HALF, HALF)]

    for half in (0, 1):
        dst = piece(own.at[low, quarter], half)
        sem = recv_x.at[low, quarter, half]
        for i, ref in enumerate(inputs):
            keep = pltpu.make_async_copy(piece(ref, half), dst, sem)
            give = remote(piece(ref, half), dst, send_x.at[0], sem, sibling)
            pl.when(core == i)(keep.start)
            pl.when(core != i)(give.start)
    first = jnp.where(core == low, other, pair)
    second = jnp.where(core == low, pair, other)

    def x_send(n, half):
        for i, ref in enumerate(inputs):
            copy = remote(
                piece(ref, half), piece(own.at[low, quarter], half),
                send_x.at[1], recv_x.at[low, quarter, half],
                at_x(second if n else first, i),
            )
            copy.start()

    kept = []
    for half in (0, 1):
        for i, ref in enumerate(inputs):
            copy = remote(
                piece(ref, half), piece(ring.at[0, low], half),
                send_y.at[0], recv_y.at[0, low, half],
                place(y_up if i else y_down, h, i, low, z),
            )
            pl.when(core == low)(copy.start)
    x_send(0, 0)
    x_send(0, 1)

    def slot_of(chip, k):
        return lax.rem(chip, 2), 2 * lax.div(chip, 2) + k

    def arrive(chip, k, half):
        lo, qq = slot_of(chip, k)
        ref = piece(own.at[lo, qq], half)
        pltpu.make_async_copy(ref, ref, recv_x.at[lo, qq, half]).wait()

    def turn(chip):
        for k in (0, 1):
            lo, qq = slot_of(chip, k)
            turned[lo, qq] = own[lo, qq].T

    def pass_on(half, origin, k, to, n):
        lo, qq = slot_of(origin, k)
        ref = piece(own.at[lo, qq], half)
        copy = remote(ref, ref, send_x.at[2], recv_x.at[lo, qq, half], at_x(to, core))
        copy.start()

    q = 2 * h + low
    y_next = jnp.where(core == 0, y_down, y_up)
    groups = (low, 1 - low)

    def ring_piece(step, n, half):
        lo = groups[n]
        if step < 0:
            return piece(own.at[lo, q], half)
        return piece(ring.at[step, lo], half)

    def ring_wait(step, n, half):
        ref = ring_piece(step, n, half)
        pltpu.make_async_copy(ref, ref, recv_y.at[step, groups[n], half]).wait()

    def y_send(step, n, half):
        if step > 0:
            ring_wait(step - 1, n, half)
        copy = remote(
            ring_piece(step - 1, n, half), ring_piece(step, n, half),
            send_y.at[min(step, 1) + 1], recv_y.at[step, groups[n], half],
            place(y_next, h, core, low, z),
        )
        copy.start()

    def rows_of(unit):
        if unit == BOTH:
            return 0, 2
        return (h if unit == NEAR else 1 - h), 1

    def product(d, unit):
        first, count = rows_of(unit)

        def term(lo):
            right = own[lo, q] if d == 0 else ring[d - 1, lo]
            left = turned[lo, pl.ds(2 * first, 2 * count)]
            left = left.reshape(2 * count * WIDE, TOKENS)
            return jnp.dot(left, right, preferred_element_type=jnp.float32)

        total = term(0) + term(1)
        part[d, pl.ds(first, count)] = total.reshape(count, 2 * WIDE, WIDE)

    def greet(n):
        for way, zz in enumerate((z_up, z_down)):
            pl.semaphore_signal(
                near.at[n, way], inc=1, device_id=place(y, h, core, low, zz),
                device_id_type=pl.DeviceIdType.MESH,
            )

    def greeted(n):
        for way in (0, 1):
            pl.semaphore_wait(near.at[n, way], 1)

    def scatter(d, unit):
        side = pl.ds(*rows_of(unit))
        term = part[d, side] * 0.0625
        square = term * term
        power = term * jnp.abs(term) * square * (square * square)
        coded[d, side] = power.astype(jnp.bfloat16)
        for o in (4, 3, 5, 2, 6, 1, 7):
            zz = lax.rem(z + o, Z)
            copy = remote(
                coded.at[d, side, pl.ds(pl.multiple_of(zz * CHUNK, CHUNK), CHUNK)],
                cbuf.at[d, o - 1, side],
                send_c.at[0], recv_c.at[d, unit],
                place(y, h, core, low, zz),
            )
            copy.start()

    def gathered(d, unit):
        side = pl.ds(*rows_of(unit))
        terms = cbuf.at[d, :, side]
        pltpu.make_async_copy(terms, terms, recv_c.at[d, unit]).wait()
        total = 0.0
        for o in range(1, Z):
            power = cbuf[d, o - 1, side].astype(jnp.float32)
            root = jnp.sqrt(jnp.sqrt(jnp.sqrt(jnp.abs(power))))
            total += jnp.where(power < 0.0, -root, root)
        return total * 16.0


    def deliver(d, unit):
        first, count = rows_of(unit)
        mine = part.at[d]
        here = pl.ds(pl.multiple_of(z * CHUNK, CHUNK), CHUNK)
        mine[pl.ds(first, count), here, :] += gathered(d, unit)
        yq = lax.rem(y + Y + jnp.where(core == 0, d, -d), Y)
        t1 = 2 * yq + h
        kk, row = lax.div(z, 4), lax.rem(z, 4) * CHUNK
        for n in range(count):
            a = first + n
            dst = direct.at[
                core,
                pl.ds(pl.multiple_of(row, CHUNK), CHUNK),
                pl.ds(pl.multiple_of(low * WIDE, WIDE), WIDE),
            ]
            is_self = (a == h) & (kk == core) & (t1 == tok)
            copy = remote(
                mine.at[a, here], dst, send_d.at[2 * d + unit % 2 + n], recv_d.at[core],
                place(y, a, kk, lax.div(t1, Z), lax.rem(t1, Z)),
            )
            local = pltpu.make_async_copy(mine.at[a, here], dst, recv_d.at[core])
            pl.when(jnp.logical_not(is_self))(copy.start)
            pl.when(is_self)(local.start)
            kept.append((jnp.logical_not(is_self), copy))
            if 0 < d < 4:
                t2 = 2 * y + a
                copy = remote(
                    mine.at[a, here],
                    mirror.at[core, here],
                    send_d.at[10], recv_d.at[core],
                    place(yq, h, low, lax.div(t2, Z), lax.rem(t2, Z)),
                )
                copy.start()

    greet(0)
    arrive(x, low, 0)
    arrive(x, low, 1)
    arrive(x, 1 - low, 0)
    arrive(x, 1 - low, 1)
    turn(x)
    arrive(pair, low, 0)
    greeted(0)
    greet(1)
    y_send(0, 1, 0)
    x_send(1, 0)
    pass_on(0, pair, low, other, 5)
    arrive(other, 1 - low, 0)
    pass_on(0, other, 1 - low, pair, 6)
    y_send(1, 0, 0)
    y_send(1, 0, 1)
    arrive(pair, low, 1)
    y_send(0, 1, 1)
    x_send(1, 1)
    pass_on(1, pair, low, other, 5)
    arrive(other, 1 - low, 1)
    greeted(1)
    greet(2)
    pass_on(1, other, 1 - low, pair, 6)
    y_send(1, 1, 0)
    y_send(2, 0, 0)
    y_send(2, 0, 1)
    y_send(1, 1, 1)
    y_send(2, 1, 0)
    y_send(3, 0, 0)
    arrive(pair, 1 - low, 0)
    arrive(pair, 1 - low, 1)
    turn(pair)
    greeted(2)
    product(0, NEAR)
    scatter(0, NEAR)
    product(1, NEAR)
    scatter(1, NEAR)
    y_send(3, 0, 1)
    y_send(2, 1, 1)
    product(2, NEAR)
    scatter(2, NEAR)
    arrive(other, low, 0)
    arrive(other, low, 1)
    turn(other)
    arrive(far, low, 0)
    arrive(far, low, 1)
    arrive(far, 1 - low, 0)
    arrive(far, 1 - low, 1)
    turn(far)
    product(0, FAR)
    scatter(0, FAR)
    y_send(3, 1, 0)
    y_send(3, 1, 1)
    product(1, FAR)
    scatter(1, FAR)
    product(2, FAR)
    scatter(2, FAR)
    product(3, BOTH)
    scatter(3, BOTH)
    ring_wait(3, 0, 0)
    ring_wait(3, 0, 1)
    ring_wait(3, 1, 0)
    ring_wait(3, 1, 1)
    product(4, BOTH)
    scatter(4, BOTH)
    deliver(0, NEAR)
    deliver(1, NEAR)
    deliver(2, NEAR)
    deliver(0, FAR)
    deliver(1, FAR)
    deliver(2, FAR)
    deliver(3, BOTH)
    deliver(4, BOTH)

    scale = jnp.float32(1.0 / (TOKENS * 2 * Z))
    y2 = lax.div(tok, 2)
    for i, out in enumerate((out_a, out_g)):
        d = lax.rem((y2 - y if i == 0 else y - y2) + Y, Y)
        straight = d <= 4

        @pl.when(straight)
        def _():
            ref = direct.at[i]
            pltpu.make_async_copy(ref, ref, recv_d.at[i]).wait()
            out[...] = direct[i] * scale

        @pl.when(jnp.logical_not(straight))
        def _():
            ref = mirror.at[i]
            pltpu.make_async_copy(ref, ref, recv_d.at[i]).wait()
            out[...] = mirror[i].T * scale

    def all_left(ref, sem):
        pltpu.make_async_copy(ref, ref, sem).wait()

    all_left(own.at[0, 0], send_x.at[0])
    all_left(own.at[0], send_x.at[1])
    all_left(own.at[0, pl.ds(0, 2)], send_x.at[2])
    pl.when(core == low)(lambda: all_left(ring.at[0], send_y.at[0]))
    all_left(ring.at[0, 0], send_y.at[1])
    all_left(ring.at[pl.ds(0, 3)], send_y.at[2])
    all_left(cbuf, send_c.at[0])
    all_left(mirror.at[0, pl.ds(0, 6 * CHUNK)], send_d.at[10])
    for remote_one, copy in kept:
        pl.when(remote_one)(copy.wait_send)


def per_device(activations, gradients):
    vmem, sem = pltpu.VMEM, pltpu.SemaphoreType.DMA
    block = jax.ShapeDtypeStruct((WIDE, 2 * WIDE), jnp.float32)
    return pl.pallas_call(
        kernel,
        out_shape=(block, block),
        in_specs=[pl.BlockSpec(memory_space=pl.ANY)] * 2,
        out_specs=[pl.BlockSpec(memory_space=pltpu.VMEM)] * 2,
        scratch_shapes=[
            vmem((2, 4, TOKENS, WIDE), jnp.bfloat16),
            vmem((2, 4, WIDE, TOKENS), jnp.bfloat16),
            vmem((4, 2, TOKENS, WIDE), jnp.bfloat16),
            vmem((5, 2, 2 * WIDE, WIDE), jnp.float32),
            vmem((5, 2, 2 * WIDE, WIDE), jnp.bfloat16),
            vmem((5, 7, 2, CHUNK, WIDE), jnp.bfloat16),
            vmem((2, WIDE, 2 * WIDE), jnp.float32),
            vmem((2, 2 * WIDE, WIDE), jnp.float32),
            sem((3,)), sem((2, 4, 2)),
            sem((3,)), sem((4, 2, 2)),
            pltpu.SemaphoreType.REGULAR((3, 2)),
            sem((1,)), sem((5, 3)),
            sem((11,)), sem((2,)),
        ],
        compiler_params=pltpu.CompilerParams(
            collective_id=0, has_side_effects=True, vmem_limit_bytes=54840 * 2**10
        ),
        cost_estimate=pl.CostEstimate(
            flops=2 * 2560 * 1536 * 128, bytes_accessed=2**20, transcendentals=0
        ),
    )(activations, gradients)


def solution(mesh):
    placed = (P("tok", "tp"), P("tok", "tp"))
    return jax.shard_map(
        per_device,
        mesh=mesh,
        in_specs=placed,
        out_specs=(P("tp", "tok"), P("tp", "tok")),
        check_vma=False,
    )
```

```python
import jax
import jax.numpy as jnp
from jax import lax
from jax.experimental import pallas as pl
from jax.experimental.pallas import tpu as pltpu
from jax.sharding import PartitionSpec as P

TOKENS = 768
WIDE = 128
HALF = TOKENS // 2
NEAR, FAR, BOTH = 0, 1, 2
CHUNK = 32
Y = 8
Z = 8


def place(y, h, core, low, z):
    return (low * Z + z, (y * 2 + h) * 2 + core)


def kernel(
    act, grad, out_a, out_g,
    own, turned, ring, part, coded, cbuf, direct, mirror,
    send_x, recv_x, send_y, recv_y, near, send_c, recv_c, send_d, recv_d,
):
    tok, tp = lax.axis_index("tok"), lax.axis_index("tp")
    low, z = lax.div(tok, Z), lax.rem(tok, Z)
    y, h, core = lax.div(tp, 4), lax.rem(lax.div(tp, 2), 2), lax.rem(tp, 2)
    x = 2 * h + low

    def remote(src, dst, send, recv, device):
        return pltpu.make_async_remote_copy(
            src_ref=src, dst_ref=dst, send_sem=send, recv_sem=recv,
            device_id=device, device_id_type=pl.DeviceIdType.MESH,
        )

    def at_x(xx, cc):
        return place(y, lax.div(xx, 2), cc, lax.rem(xx, 2), z)

    x_up, x_down = lax.rem(x + 1, 4), lax.rem(x + 3, 4)
    y_up, y_down = lax.rem(y + 1, Y), lax.rem(y + Y - 1, Y)
    z_up, z_down = lax.rem(z + 1, Z), lax.rem(z + Z - 1, Z)
    sibling = place(y, h, 1 - core, low, z)

    barrier = pltpu.get_barrier_semaphore()
    partners = [sibling]
    partners += [at_x(xx, cc) for xx in (x_up, x_down) for cc in (0, 1)]
    partners += [place(yy, h, cc, low, z) for yy in (y_up, y_down) for cc in (0, 1)]
    partners += [place(y, h, core, low, zz) for zz in (z_up, z_down)]
    for partner in partners:
        pl.semaphore_signal(
            barrier, inc=1, device_id=partner, device_id_type=pl.DeviceIdType.MESH
        )
    pl.semaphore_wait(barrier, len(partners))

    quarter = 2 * h + core
    pair = 2 * h + 1 - low
    other = lax.rem(x + 3 + 2 * low, 4)
    far = lax.rem(x + 2, 4)
    inputs = (act, grad)

    def piece(ref, part_of):
        return ref.at[pl.ds(part_of * HALF, HALF)]

    for half in (0, 1):
        dst = piece(own.at[low, quarter], half)
        sem = recv_x.at[low, quarter, half]
        for i, ref in enumerate(inputs):
            keep = pltpu.make_async_copy(piece(ref, half), dst, sem)
            give = remote(piece(ref, half), dst, send_x.at[0], sem, sibling)
            pl.when(core == i)(keep.start)
            pl.when(core != i)(give.start)
    first = jnp.where(core == low, other, pair)
    second = jnp.where(core == low, pair, other)

    def x_send(n, half):
        for i, ref in enumerate(inputs):
            copy = remote(
                piece(ref, half), piece(own.at[low, quarter], half),
                send_x.at[1], recv_x.at[low, quarter, half],
                at_x(second if n else first, i),
            )
            copy.start()

    kept = []
    for half in (0, 1):
        for i, ref in enumerate(inputs):
            copy = remote(
                piece(ref, half), piece(ring.at[0, low], half),
                send_y.at[0], recv_y.at[0, low, half],
                place(y_up if i else y_down, h, i, low, z),
            )
            pl.when(core == low)(copy.start)
    x_send(0, 0)
    x_send(0, 1)

    def slot_of(chip, k):
        return lax.rem(chip, 2), 2 * lax.div(chip, 2) + k

    def arrive(chip, k, half):
        lo, qq = slot_of(chip, k)
        ref = piece(own.at[lo, qq], half)
        pltpu.make_async_copy(ref, ref, recv_x.at[lo, qq, half]).wait()

    def turn(chip):
        for k in (0, 1):
            lo, qq = slot_of(chip, k)
            turned[lo, qq] = own[lo, qq].T

    def pass_on(half, origin, k, to, n):
        lo, qq = slot_of(origin, k)
        ref = piece(own.at[lo, qq], half)
        copy = remote(ref, ref, send_x.at[2], recv_x.at[lo, qq, half], at_x(to, core))
        copy.start()

    q = 2 * h + low
    y_next = jnp.where(core == 0, y_down, y_up)
    groups = (low, 1 - low)

    def ring_piece(step, n, half):
        lo = groups[n]
        if step < 0:
            return piece(own.at[lo, q], half)
        return piece(ring.at[step, lo], half)

    def ring_wait(step, n, half):
        ref = ring_piece(step, n, half)
        pltpu.make_async_copy(ref, ref, recv_y.at[step, groups[n], half]).wait()

    def y_send(step, n, half):
        if step > 0:
            ring_wait(step - 1, n, half)
        copy = remote(
            ring_piece(step - 1, n, half), ring_piece(step, n, half),
            send_y.at[min(step, 1) + 1], recv_y.at[step, groups[n], half],
            place(y_next, h, core, low, z),
        )
        copy.start()

    def rows_of(unit):
        if unit == BOTH:
            return 0, 2
        return (h if unit == NEAR else 1 - h), 1

    def product(d, unit):
        first, count = rows_of(unit)

        def term(lo):
            right = own[lo, q] if d == 0 else ring[d - 1, lo]
            left = turned[lo, pl.ds(2 * first, 2 * count)]
            left = left.reshape(2 * count * WIDE, TOKENS)
            return jnp.dot(left, right, preferred_element_type=jnp.float32)

        total = term(groups[0])
        if d == 4:
            ring_wait(3, 1, 0)
            ring_wait(3, 1, 1)
        total += term(groups[1])
        part[d, pl.ds(first, count)] = total.reshape(count, 2 * WIDE, WIDE)

    def greet(n):
        for way, zz in enumerate((z_up, z_down)):
            pl.semaphore_signal(
                near.at[n, way], inc=1, device_id=place(y, h, core, low, zz),
                device_id_type=pl.DeviceIdType.MESH,
            )

    def greeted(n):
        for way in (0, 1):
            pl.semaphore_wait(near.at[n, way], 1)

    def scatter(d, unit):
        side = pl.ds(*rows_of(unit))
        term = part[d, side] * 0.0625
        square = term * term
        power = term * jnp.abs(term) * square * (square * square)
        coded[d, side] = power.astype(jnp.bfloat16)
        for o in (4, 3, 5, 2, 6, 1, 7):
            zz = lax.rem(z + o, Z)
            copy = remote(
                coded.at[d, side, pl.ds(pl.multiple_of(zz * CHUNK, CHUNK), CHUNK)],
                cbuf.at[d, o - 1, side],
                send_c.at[0], recv_c.at[d + 5 * (unit % 2)],
                place(y, h, core, low, zz),
            )
            copy.start()

    def gathered(d, unit):
        side = pl.ds(*rows_of(unit))
        terms = cbuf.at[d, :, side]
        pltpu.make_async_copy(terms, terms, recv_c.at[d + 5 * (unit % 2)]).wait()
        total = 0.0
        for o in range(1, Z):
            power = cbuf[d, o - 1, side].astype(jnp.float32)
            root = jnp.sqrt(jnp.sqrt(jnp.sqrt(jnp.abs(power))))
            total += jnp.where(power < 0.0, -root, root)
        return total * 16.0


    def deliver(d, unit):
        first, count = rows_of(unit)
        mine = part.at[d]
        here = pl.ds(pl.multiple_of(z * CHUNK, CHUNK), CHUNK)
        mine[pl.ds(first, count), here, :] += gathered(d, unit)
        yq = lax.rem(y + Y + jnp.where(core == 0, d, -d), Y)
        t1 = 2 * yq + h
        kk, row = lax.div(z, 4), lax.rem(z, 4) * CHUNK
        for n in range(count):
            a = first + n
            dst = direct.at[
                core,
                pl.ds(pl.multiple_of(row, CHUNK), CHUNK),
                pl.ds(pl.multiple_of(low * WIDE, WIDE), WIDE),
            ]
            is_self = (a == h) & (kk == core) & (t1 == tok)
            copy = remote(
                mine.at[a, here], dst, send_d.at[2 * d + unit % 2 + n], recv_d.at[core],
                place(y, a, kk, lax.div(t1, Z), lax.rem(t1, Z)),
            )
            local = pltpu.make_async_copy(mine.at[a, here], dst, recv_d.at[core])
            pl.when(jnp.logical_not(is_self))(copy.start)
            pl.when(is_self)(local.start)
            kept.append((jnp.logical_not(is_self), copy))
            if 0 < d < 4:
                t2 = 2 * y + a
                copy = remote(
                    mine.at[a, here],
                    mirror.at[core, here],
                    send_d.at[10], recv_d.at[core],
                    place(yq, h, low, lax.div(t2, Z), lax.rem(t2, Z)),
                )
                copy.start()

    greet(0)
    arrive(x, low, 0)
    arrive(x, low, 1)
    arrive(x, 1 - low, 0)
    arrive(x, 1 - low, 1)
    turn(x)
    arrive(pair, low, 0)
    greeted(0)
    greet(1)
    y_send(0, 1, 0)
    x_send(1, 0)
    pass_on(0, pair, low, other, 5)
    arrive(other, 1 - low, 0)
    pass_on(0, other, 1 - low, pair, 6)
    y_send(1, 0, 0)
    y_send(1, 0, 1)
    arrive(pair, low, 1)
    y_send(0, 1, 1)
    x_send(1, 1)
    pass_on(1, pair, low, other, 5)
    arrive(other, 1 - low, 1)
    greeted(1)
    greet(2)
    pass_on(1, other, 1 - low, pair, 6)
    y_send(1, 1, 0)
    y_send(2, 0, 0)
    y_send(2, 0, 1)
    y_send(1, 1, 1)
    y_send(2, 1, 0)
    y_send(3, 0, 0)
    arrive(pair, 1 - low, 0)
    arrive(pair, 1 - low, 1)
    turn(pair)
    greeted(2)
    product(0, NEAR)
    scatter(0, NEAR)
    product(1, NEAR)
    scatter(1, NEAR)
    y_send(3, 0, 1)
    y_send(2, 1, 1)
    product(2, NEAR)
    scatter(2, NEAR)
    arrive(other, low, 0)
    arrive(other, low, 1)
    turn(other)
    arrive(far, low, 0)
    arrive(far, low, 1)
    arrive(far, 1 - low, 0)
    arrive(far, 1 - low, 1)
    turn(far)
    product(0, FAR)
    scatter(0, FAR)
    y_send(3, 1, 0)
    y_send(3, 1, 1)
    product(1, FAR)
    scatter(1, FAR)
    product(2, FAR)
    scatter(2, FAR)
    product(3, BOTH)
    scatter(3, BOTH)
    ring_wait(3, 0, 0)
    ring_wait(3, 0, 1)
    product(4, BOTH)
    scatter(4, BOTH)
    deliver(2, NEAR)
    deliver(2, FAR)
    deliver(1, NEAR)
    deliver(1, FAR)
    deliver(3, BOTH)
    deliver(0, NEAR)
    deliver(0, FAR)
    deliver(4, BOTH)

    scale = jnp.float32(1.0 / (TOKENS * 2 * Z))
    y2 = lax.div(tok, 2)
    for i, out in enumerate((out_a, out_g)):
        d = lax.rem((y2 - y if i == 0 else y - y2) + Y, Y)
        straight = d <= 4

        @pl.when(straight)
        def _():
            ref = direct.at[i]
            pltpu.make_async_copy(ref, ref, recv_d.at[i]).wait()
            out[...] = direct[i] * scale

        @pl.when(jnp.logical_not(straight))
        def _():
            ref = mirror.at[i]
            pltpu.make_async_copy(ref, ref, recv_d.at[i]).wait()
            out[...] = mirror[i].T * scale

    def all_left(ref, sem):
        pltpu.make_async_copy(ref, ref, sem).wait()

    all_left(own.at[0, 0], send_x.at[0])
    all_left(own.at[0], send_x.at[1])
    all_left(own.at[0, pl.ds(0, 2)], send_x.at[2])
    pl.when(core == low)(lambda: all_left(ring.at[0], send_y.at[0]))
    all_left(ring.at[0, 0], send_y.at[1])
    all_left(ring.at[pl.ds(0, 3)], send_y.at[2])
    all_left(cbuf, send_c.at[0])
    all_left(mirror.at[0, pl.ds(0, 6 * CHUNK)], send_d.at[10])
    for remote_one, copy in kept:
        pl.when(remote_one)(copy.wait_send)


def per_device(activations, gradients):
    vmem, sem = pltpu.VMEM, pltpu.SemaphoreType.DMA
    block = jax.ShapeDtypeStruct((WIDE, 2 * WIDE), jnp.float32)
    return pl.pallas_call(
        kernel,
        out_shape=(block, block),
        in_specs=[pl.BlockSpec(memory_space=pl.ANY)] * 2,
        out_specs=[pl.BlockSpec(memory_space=pltpu.VMEM)] * 2,
        scratch_shapes=[
            vmem((2, 4, TOKENS, WIDE), jnp.bfloat16),
            vmem((2, 4, WIDE, TOKENS), jnp.bfloat16),
            vmem((4, 2, TOKENS, WIDE), jnp.bfloat16),
            vmem((5, 2, 2 * WIDE, WIDE), jnp.float32),
            vmem((5, 2, 2 * WIDE, WIDE), jnp.bfloat16),
            vmem((5, 7, 2, CHUNK, WIDE), jnp.bfloat16),
            vmem((2, WIDE, 2 * WIDE), jnp.float32),
            vmem((2, 2 * WIDE, WIDE), jnp.float32),
            sem((3,)), sem((2, 4, 2)),
            sem((3,)), sem((4, 2, 2)),
            pltpu.SemaphoreType.REGULAR((3, 2)),
            sem((1,)), sem((8,)),
            sem((11,)), sem((2,)),
        ],
        compiler_params=pltpu.CompilerParams(
            collective_id=0, has_side_effects=True, vmem_limit_bytes=54840 * 2**10
        ),
        cost_estimate=pl.CostEstimate(
            flops=2 * 2560 * 1536 * 128, bytes_accessed=2**20, transcendentals=0
        ),
    )(activations, gradients)


def solution(mesh):
    placed = (P("tok", "tp"), P("tok", "tp"))
    return jax.shard_map(
        per_device,
        mesh=mesh,
        in_specs=placed,
        out_specs=(P("tp", "tok"), P("tp", "tok")),
        check_vma=False,
    )
```

```python
import jax
import jax.numpy as jnp
from jax import lax
from jax.experimental import pallas as pl
from jax.experimental.pallas import tpu as pltpu
from jax.sharding import PartitionSpec as P

TOKENS = 768
WIDE = 128
HALF = TOKENS // 2
NEAR, FAR, BOTH = 0, 1, 2
CHUNK = 32
Y = 8
Z = 8


def place(y, h, core, low, z):
    return (low * Z + z, (y * 2 + h) * 2 + core)


def kernel(
    act, grad, out_a, out_g,
    own, turned, ring, part, coded, cbuf, direct, mirror,
    send_x, recv_x, send_y, recv_y, near, send_c, recv_c, send_d, recv_d,
):
    tok, tp = lax.axis_index("tok"), lax.axis_index("tp")
    low, z = lax.div(tok, Z), lax.rem(tok, Z)
    y, h, core = lax.div(tp, 4), lax.rem(lax.div(tp, 2), 2), lax.rem(tp, 2)
    x = 2 * h + low

    def remote(src, dst, send, recv, device):
        return pltpu.make_async_remote_copy(
            src_ref=src, dst_ref=dst, send_sem=send, recv_sem=recv,
            device_id=device, device_id_type=pl.DeviceIdType.MESH,
        )

    def at_x(xx, cc):
        return place(y, lax.div(xx, 2), cc, lax.rem(xx, 2), z)

    x_up, x_down = lax.rem(x + 1, 4), lax.rem(x + 3, 4)
    y_up, y_down = lax.rem(y + 1, Y), lax.rem(y + Y - 1, Y)
    z_up, z_down = lax.rem(z + 1, Z), lax.rem(z + Z - 1, Z)
    sibling = place(y, h, 1 - core, low, z)

    barrier = pltpu.get_barrier_semaphore()
    partners = [sibling]
    partners += [at_x(xx, cc) for xx in (x_up, x_down) for cc in (0, 1)]
    partners += [place(yy, h, cc, low, z) for yy in (y_up, y_down) for cc in (0, 1)]
    partners += [place(y, h, core, low, zz) for zz in (z_up, z_down)]
    for partner in partners:
        pl.semaphore_signal(
            barrier, inc=1, device_id=partner, device_id_type=pl.DeviceIdType.MESH
        )
    pl.semaphore_wait(barrier, len(partners))

    quarter = 2 * h + core
    pair = 2 * h + 1 - low
    other = lax.rem(x + 3 + 2 * low, 4)
    far = lax.rem(x + 2, 4)
    inputs = (act, grad)

    def piece(ref, part_of):
        return ref.at[pl.ds(part_of * HALF, HALF)]

    for half in (0, 1):
        dst = piece(own.at[low, quarter], half)
        sem = recv_x.at[low, quarter, half]
        for i, ref in enumerate(inputs):
            keep = pltpu.make_async_copy(piece(ref, half), dst, sem)
            give = remote(piece(ref, half), dst, send_x.at[0], sem, sibling)
            pl.when(core == i)(keep.start)
            pl.when(core != i)(give.start)
    first = jnp.where(core == low, other, pair)
    second = jnp.where(core == low, pair, other)

    def x_send(n, half):
        for i, ref in enumerate(inputs):
            copy = remote(
                piece(ref, half), piece(own.at[low, quarter], half),
                send_x.at[1], recv_x.at[low, quarter, half],
                at_x(second if n else first, i),
            )
            copy.start()

    kept = []
    for half in (0, 1):
        for i, ref in enumerate(inputs):
            copy = remote(
                piece(ref, half), piece(ring.at[0, low], half),
                send_y.at[0], recv_y.at[0, low, half],
                place(y_up if i else y_down, h, i, low, z),
            )
            pl.when(core == low)(copy.start)
    x_send(0, 0)
    x_send(0, 1)

    def slot_of(chip, k):
        return lax.rem(chip, 2), 2 * lax.div(chip, 2) + k

    def arrive(chip, k, half):
        lo, qq = slot_of(chip, k)
        ref = piece(own.at[lo, qq], half)
        pltpu.make_async_copy(ref, ref, recv_x.at[lo, qq, half]).wait()

    def turn(chip):
        for k in (0, 1):
            lo, qq = slot_of(chip, k)
            turned[lo, qq] = own[lo, qq].T

    def pass_on(half, origin, k, to, n):
        lo, qq = slot_of(origin, k)
        ref = piece(own.at[lo, qq], half)
        copy = remote(ref, ref, send_x.at[2], recv_x.at[lo, qq, half], at_x(to, core))
        copy.start()

    q = 2 * h + low
    y_next = jnp.where(core == 0, y_down, y_up)
    groups = (low, 1 - low)

    def ring_piece(step, n, half):
        lo = groups[n]
        if step < 0:
            return piece(own.at[lo, q], half)
        return piece(ring.at[step, lo], half)

    def ring_wait(step, n, half):
        ref = ring_piece(step, n, half)
        pltpu.make_async_copy(ref, ref, recv_y.at[step, groups[n], half]).wait()

    def y_send(step, n, half):
        if step > 0:
            ring_wait(step - 1, n, half)
        copy = remote(
            ring_piece(step - 1, n, half), ring_piece(step, n, half),
            send_y.at[min(step, 1) + 1], recv_y.at[step, groups[n], half],
            place(y_next, h, core, low, z),
        )
        copy.start()

    def rows_of(unit):
        if unit == BOTH:
            return 0, 2
        return (h if unit == NEAR else 1 - h), 1

    def product(d, unit):
        first, count = rows_of(unit)

        def term(lo):
            right = own[lo, q] if d == 0 else ring[d - 1, lo]
            left = turned[lo, pl.ds(2 * first, 2 * count)]
            left = left.reshape(2 * count * WIDE, TOKENS)
            return jnp.dot(left, right, preferred_element_type=jnp.float32)

        total = term(groups[0])
        if d == 4:
            ring_wait(3, 1, 0)
            ring_wait(3, 1, 1)
        total += term(groups[1])
        part[d, pl.ds(first, count)] = total.reshape(count, 2 * WIDE, WIDE)

    def greet(n):
        for way, zz in enumerate((z_up, z_down)):
            pl.semaphore_signal(
                near.at[n, way], inc=1, device_id=place(y, h, core, low, zz),
                device_id_type=pl.DeviceIdType.MESH,
            )

    def greeted(n):
        for way in (0, 1):
            pl.semaphore_wait(near.at[n, way], 1)

    def scatter(d, unit):
        side = pl.ds(*rows_of(unit))
        term = part[d, side] * 0.0625
        square = term * term
        power = term * jnp.abs(term) * square * (square * square)
        coded[d, side] = power.astype(jnp.bfloat16)
        for o in (4, 3, 5, 2, 6, 1, 7):
            zz = lax.rem(z + o, Z)
            copy = remote(
                coded.at[d, side, pl.ds(pl.multiple_of(zz * CHUNK, CHUNK), CHUNK)],
                cbuf.at[d, o - 1, side],
                send_c.at[0], recv_c.at[d + 5 * (unit % 2)],
                place(y, h, core, low, zz),
            )
            copy.start()

    def gathered(d, unit):
        side = pl.ds(*rows_of(unit))
        terms = cbuf.at[d, :, side]
        pltpu.make_async_copy(terms, terms, recv_c.at[d + 5 * (unit % 2)]).wait()
        total = 0.0
        for o in range(1, Z):
            power = cbuf[d, o - 1, side].astype(jnp.float32)
            root = jnp.sqrt(jnp.sqrt(jnp.sqrt(jnp.abs(power))))
            total += jnp.where(power < 0.0, -root, root)
        return total * 16.0


    def deliver(d, unit):
        first, count = rows_of(unit)
        mine = part.at[d]
        here = pl.ds(pl.multiple_of(z * CHUNK, CHUNK), CHUNK)
        mine[pl.ds(first, count), here, :] += gathered(d, unit)
        yq = lax.rem(y + Y + jnp.where(core == 0, d, -d), Y)
        t1 = 2 * yq + h
        kk, row = lax.div(z, 4), lax.rem(z, 4) * CHUNK
        for n in range(count):
            a = first + n
            if 0 < d < 4:
                t2 = 2 * y + a
                copy = remote(
                    mine.at[a, here],
                    mirror.at[core, here],
                    send_d.at[10], recv_d.at[core],
                    place(yq, h, low, lax.div(t2, Z), lax.rem(t2, Z)),
                )
                copy.start()
        for n in range(count):
            a = first + n
            dst = direct.at[
                core,
                pl.ds(pl.multiple_of(row, CHUNK), CHUNK),
                pl.ds(pl.multiple_of(low * WIDE, WIDE), WIDE),
            ]
            is_self = (a == h) & (kk == core) & (t1 == tok)
            copy = remote(
                mine.at[a, here], dst, send_d.at[2 * d + unit % 2 + n], recv_d.at[core],
                place(y, a, kk, lax.div(t1, Z), lax.rem(t1, Z)),
            )
            local = pltpu.make_async_copy(mine.at[a, here], dst, recv_d.at[core])
            pl.when(jnp.logical_not(is_self))(copy.start)
            pl.when(is_self)(local.start)
            kept.append((jnp.logical_not(is_self), copy))

    greet(0)
    arrive(x, low, 0)
    arrive(x, low, 1)
    arrive(x, 1 - low, 0)
    arrive(x, 1 - low, 1)
    turn(x)
    arrive(pair, low, 0)
    greeted(0)
    greet(1)
    y_send(0, 1, 0)
    x_send(1, 0)
    pass_on(0, pair, low, other, 5)
    arrive(other, 1 - low, 0)
    pass_on(0, other, 1 - low, pair, 6)
    y_send(1, 0, 0)
    y_send(1, 0, 1)
    arrive(pair, low, 1)
    y_send(0, 1, 1)
    x_send(1, 1)
    pass_on(1, pair, low, other, 5)
    arrive(other, 1 - low, 1)
    greeted(1)
    greet(2)
    pass_on(1, other, 1 - low, pair, 6)
    y_send(1, 1, 0)
    y_send(2, 0, 0)
    y_send(2, 0, 1)
    y_send(1, 1, 1)
    y_send(2, 1, 0)
    y_send(3, 0, 0)
    arrive(pair, 1 - low, 0)
    arrive(pair, 1 - low, 1)
    turn(pair)
    greeted(2)
    product(0, NEAR)
    scatter(0, NEAR)
    product(1, NEAR)
    scatter(1, NEAR)
    y_send(3, 0, 1)
    y_send(2, 1, 1)
    product(2, NEAR)
    scatter(2, NEAR)
    arrive(other, low, 0)
    arrive(other, low, 1)
    turn(other)
    arrive(far, low, 0)
    arrive(far, low, 1)
    arrive(far, 1 - low, 0)
    arrive(far, 1 - low, 1)
    turn(far)
    product(0, FAR)
    scatter(0, FAR)
    y_send(3, 1, 0)
    y_send(3, 1, 1)
    product(1, FAR)
    scatter(1, FAR)
    product(2, FAR)
    scatter(2, FAR)
    product(3, BOTH)
    scatter(3, BOTH)
    ring_wait(3, 0, 0)
    ring_wait(3, 0, 1)
    product(4, BOTH)
    scatter(4, BOTH)
    deliver(2, NEAR)
    deliver(2, FAR)
    deliver(1, NEAR)
    deliver(1, FAR)
    deliver(3, BOTH)
    deliver(0, NEAR)
    deliver(0, FAR)
    deliver(4, BOTH)

    scale = jnp.float32(1.0 / (TOKENS * 2 * Z))
    y2 = lax.div(tok, 2)
    for i, out in enumerate((out_a, out_g)):
        d = lax.rem((y2 - y if i == 0 else y - y2) + Y, Y)
        straight = d <= 4

        @pl.when(straight)
        def _():
            ref = direct.at[i]
            pltpu.make_async_copy(ref, ref, recv_d.at[i]).wait()
            out[...] = direct[i] * scale

        @pl.when(jnp.logical_not(straight))
        def _():
            ref = mirror.at[i]
            pltpu.make_async_copy(ref, ref, recv_d.at[i]).wait()
            out[...] = mirror[i].T * scale

    def all_left(ref, sem):
        pltpu.make_async_copy(ref, ref, sem).wait()

    all_left(own.at[0, 0], send_x.at[0])
    all_left(own.at[0], send_x.at[1])
    all_left(own.at[0, pl.ds(0, 2)], send_x.at[2])
    pl.when(core == low)(lambda: all_left(ring.at[0], send_y.at[0]))
    all_left(ring.at[0, 0], send_y.at[1])
    all_left(ring.at[pl.ds(0, 3)], send_y.at[2])
    all_left(cbuf, send_c.at[0])
    all_left(mirror.at[0, pl.ds(0, 6 * CHUNK)], send_d.at[10])
    for remote_one, copy in kept:
        pl.when(remote_one)(copy.wait_send)


def per_device(activations, gradients):
    vmem, sem = pltpu.VMEM, pltpu.SemaphoreType.DMA
    block = jax.ShapeDtypeStruct((WIDE, 2 * WIDE), jnp.float32)
    return pl.pallas_call(
        kernel,
        out_shape=(block, block),
        in_specs=[pl.BlockSpec(memory_space=pl.ANY)] * 2,
        out_specs=[pl.BlockSpec(memory_space=pltpu.VMEM)] * 2,
        scratch_shapes=[
            vmem((2, 4, TOKENS, WIDE), jnp.bfloat16),
            vmem((2, 4, WIDE, TOKENS), jnp.bfloat16),
            vmem((4, 2, TOKENS, WIDE), jnp.bfloat16),
            vmem((5, 2, 2 * WIDE, WIDE), jnp.float32),
            vmem((5, 2, 2 * WIDE, WIDE), jnp.bfloat16),
            vmem((5, 7, 2, CHUNK, WIDE), jnp.bfloat16),
            vmem((2, WIDE, 2 * WIDE), jnp.float32),
            vmem((2, 2 * WIDE, WIDE), jnp.float32),
            sem((3,)), sem((2, 4, 2)),
            sem((3,)), sem((4, 2, 2)),
            pltpu.SemaphoreType.REGULAR((3, 2)),
            sem((1,)), sem((8,)),
            sem((11,)), sem((2,)),
        ],
        compiler_params=pltpu.CompilerParams(
            collective_id=0, has_side_effects=True, vmem_limit_bytes=54840 * 2**10
        ),
        cost_estimate=pl.CostEstimate(
            flops=2 * 2560 * 1536 * 128, bytes_accessed=2**20, transcendentals=0
        ),
    )(activations, gradients)


def solution(mesh):
    placed = (P("tok", "tp"), P("tok", "tp"))
    return jax.shard_map(
        per_device,
        mesh=mesh,
        in_specs=placed,
        out_specs=(P("tp", "tok"), P("tp", "tok")),
        check_vma=False,
    )
```
